512 devices in a mesh: blk: 32 (over z, x_hi), uly: 16 (over y, x_lo, core).
Axes of the slice: x: 4 (x_hi: 2, x_lo: 2; x = x_hi * 2 + x_lo), y: 4, z: 16, core: 2. Of those that a mesh axis runs over, the one named last changes fastest.
Arguments:
- queries: bfloat16 [16384, 2048], P(('blk', 'uly')), may hold values from -140 to 140
- keys: bfloat16 [16384, 2048], P(('blk', 'uly')), may hold values from -5 to 5
- values: bfloat16 [16384, 2048], P(('blk', 'uly')), may hold values from -6 to 6
- tile_mask: int32 [32, 32, 4, 4], replicated, may hold values from 0 to 1, as said below
- frame_order: int32 [32], replicated, may hold values from 0 to 31, each once
Outputs:
- attended: bfloat16 [16384, 2048], P(('blk', 'uly'))
The draws below stay inside these ranges and needn't reach their ends.
Inputs may be any that keep to these rules, and one draw needn't show every extreme that they name: `tile_mask`: every tile attends the same tile of its own frame. For two different frames, exactly 2 key tiles of the key frame are attended by some query tile of the query frame. `frame_order`: each frame number appears once.
All inputs are finite; a program needn't handle non-finite values.
Results may differ from the reference program's by a relative error of at most 0.009.
Values may be sent and summed in bfloat16 or wider, within the bound.
A program may use at most 64 MiB of HBM per device.

```python
import math
import jax
import jax.numpy as jnp
from jax import lax

HD = 128
TILE = 128
FT = 4
NEED = 2
HEADS = 16
FRAMES = 32
TOKENS = 16384


def shared_keys(key):
    base_keys = jnp.clip(jax.random.normal(key, (TOKENS, HEADS * HD), jnp.float32), -5.0, 5.0)
    return base_keys


def draw_keys(key, part):
    base_keys = shared_keys(key)
    result = base_keys
    return result.astype(jnp.bfloat16)


def draw_queries(key, part):
    key = jax.random.fold_in(key, 5)
    result = jnp.clip(jax.random.normal(key, (TOKENS, HEADS * HD), jnp.float32), -5.0, 5.0)
    return result.astype(jnp.bfloat16)


def draw_tile_mask(key, part):
    key = jax.random.fold_in(key, 11)
    key_keep = jax.random.fold_in(key, 1)
    key_rank = jax.random.fold_in(key, 2)
    key_force = jax.random.fold_in(key, 3)
    query_frame = jnp.arange(FRAMES, dtype=jnp.int32)[:, None, None, None]
    key_frame = jnp.arange(FRAMES, dtype=jnp.int32)[None, :, None, None]
    query_tile = jnp.arange(FT, dtype=jnp.int32)[None, None, :, None]
    key_tile = jnp.arange(FT, dtype=jnp.int32)[None, None, None, :]
    distance = jnp.abs(query_frame - key_frame)
    level = jnp.zeros_like(distance)
    for power in range(12):
        level = level + (distance >= 1 << power).astype(jnp.int32)
    threshold = jnp.right_shift(jnp.int32(768), level)
    drawn = jax.random.randint(key_keep, (FRAMES, FRAMES, FT, FT), 0, 1024)
    keep = drawn < threshold
    rank_scores = jax.random.randint(key_rank, (FRAMES, FRAMES, FT), 0, 1 << 20) * FT + jnp.arange(FT, dtype=jnp.int32)
    order = jnp.argsort(rank_scores, axis=-1, stable=True)
    ranks = jnp.argsort(order, axis=-1, stable=True)
    chosen_key = ranks < NEED
    forced_query = jax.random.randint(key_force, (FRAMES, FRAMES, FT), 0, FT)
    forced = query_tile == forced_query[:, :, None, :]
    cross = (keep | forced) & chosen_key[:, :, None, :]
    own = keep | (query_tile == key_tile)
    return jnp.where(distance == 0, own, cross).astype(jnp.int32)


def block_scale(rng, dims, cuts, low, largest):
    def one(dim, blocks):
        steps = jax.random.uniform(jax.random.fold_in(jax.random.fold_in(rng, 6), dim), (blocks,), jnp.float32, low / len(cuts), largest / len(cuts))
        return jnp.repeat(jnp.exp(steps), dims[dim] // blocks).reshape((-1,) + (1,) * (len(dims) - dim - 1))

    gain = one(*cuts[0])
    for cut in cuts[1:]:
        gain = gain * one(*cut)
    return gain


def scatter_about(rng, extent, width, most, cuts=(), kind=jnp.bfloat16):
    values = width * jax.random.normal(rng, extent, jnp.float32)
    if cuts:
        values = values * block_scale(rng, extent, cuts, -0.22, 0.18)
    return jnp.clip(values, -most, most).astype(kind)


def setup_inputs(seed: int = 0) -> dict:
    key_of = jax.random.split(jax.random.key(seed), 6)
    queries = draw_queries(jax.random.fold_in(key_of[5], 71), 0)
    keys = draw_keys(jax.random.fold_in(key_of[5], 71), 0)
    values = scatter_about(key_of[2], (TOKENS, HEADS * HD), 1.0, 6.0, ((0, 512),))
    tile_mask = draw_tile_mask(jax.random.fold_in(key_of[5], 71), 0)
    frame_order = jax.random.permutation(key_of[4], FRAMES).astype(jnp.int32)
    return {"queries": queries, "keys": keys, "values": values, "tile_mask": tile_mask, "frame_order": frame_order}


def reference(queries, keys, values, tile_mask, frame_order):
    frame_tokens = FT * TILE
    frame_total = keys.shape[0] // frame_tokens
    score_scale = 1.0 / math.sqrt(HD)
    pair_mask = tile_mask[frame_order][:, frame_order]
    query_heads = queries.reshape(frame_total, frame_tokens, HEADS, HD).transpose(0, 2, 1, 3)
    key_heads = keys.reshape(-1, HEADS, HD).transpose(1, 0, 2)
    value_heads = values.reshape(-1, HEADS, HD).transpose(1, 0, 2)

    def per_frame(frame_args):
        frame_queries, frame_pairs = frame_args
        allowed = frame_pairs.transpose(1, 0, 2).reshape(FT, frame_total * FT) > 0
        mask_five = allowed[:, None, :, None]

        def per_head(head_args):
            head_queries, head_keys, head_values = head_args
            scores = jnp.dot(head_queries, head_keys.T, preferred_element_type=jnp.float32) * score_scale
            scores = scores.reshape(FT, TILE, frame_total * FT, TILE)
            row_max = lax.optimization_barrier(jnp.max(jnp.where(mask_five, scores, -1e+30), axis=(2, 3), keepdims=True))
            probs = jnp.where(mask_five, jnp.exp(scores - row_max), 0.0).reshape(frame_tokens, -1)
            summed = lax.optimization_barrier(jnp.sum(probs, axis=1, keepdims=True))
            mixed = jnp.dot(probs.astype(jnp.bfloat16), head_values, preferred_element_type=jnp.float32)
            return (mixed / summed).astype(jnp.bfloat16)
        return lax.map(per_head, (frame_queries, key_heads, value_heads))
    result = lax.map(per_frame, (query_heads, pair_mask))
    return result.transpose(0, 2, 1, 3).reshape(queries.shape)
```

```python
import functools
import math

import jax
import jax.numpy as jnp
from jax import lax
from jax.experimental import pallas as pl
from jax.experimental.pallas import tpu as pltpu
from jax.sharding import PartitionSpec as P

HD = 128
CH = 32
NZ = 16
GZ = 4
STEPS = NZ // GZ
MASKED = -1e30
SCALE = math.log2(math.e) / math.sqrt(HD)
MESH = pl.DeviceIdType.MESH
F32 = jnp.float32
BF16 = jnp.bfloat16


def kernel(
    q_ref, k_ref, v_ref, bias_ref, out_ref,
    qbuf, kv, acc, top, osend, lsend, orecv, lrecv, oown, lown, zsend,
    q_sent, k_sent, v_sent, q_got, kv_got, y_sent, y_got,
    x_sent, x_got, sib_got, o_sent, l_sent, o_got, l_got, r_sent, r_got,
):
    b, u = lax.axis_index("blk"), lax.axis_index("uly")
    z, xh = b // 2, b % 2
    y, xl, c = u // 4, (u // 2) % 2, u % 2
    x = xh * 2 + xl
    ahead, behind, opposite = (x + 1 + 2 * c) % 4, (x + 3 - 2 * c) % 4, (x + 2) % 4

    def dev(z2=z, x2=x, y2=y, c2=c):
        return {"blk": z2 * 2 + x2 // 2, "uly": y2 * 4 + (x2 % 2) * 2 + c2}

    def remote(src, dst, send, recv, device):
        return pltpu.make_async_remote_copy(
            src_ref=src, dst_ref=dst, send_sem=send, recv_sem=recv,
            device_id=device, device_id_type=MESH,
        )

    def wait_bytes(ref, sem):
        pltpu.make_async_copy(ref, ref, sem).wait()

    def far(i):
        mag = (i + 1) // 2
        return (z + NZ + (2 * (i % 2) - 1) * mag) % NZ

    barrier = pltpu.get_barrier_semaphore()

    def greet(i, carry):
        pl.semaphore_signal(barrier, inc=1, device_id=dev(z2=far(i)), device_id_type=MESH)
        return carry

    lax.fori_loop(1, NZ, greet, 0)
    for dy in range(1, 4):
        pl.semaphore_signal(barrier, inc=1, device_id=dev(y2=(y + dy) % 4), device_id_type=MESH)
    pl.semaphore_signal(barrier, inc=1, device_id=dev(x2=ahead), device_id_type=MESH)
    pl.semaphore_signal(barrier, inc=1, device_id=dev(x2=behind), device_id_type=MESH)
    pl.semaphore_signal(barrier, inc=1, device_id=dev(c2=1 - c), device_id_type=MESH)
    pl.semaphore_wait(barrier, NZ - 1 + 3 + 2 + 1)

    zslot = (z % 2) * (NZ // 2) + z // 2

    def cols(ref, h):
        return ref.at[:, pl.ds(pl.multiple_of(h * HD, HD), HD)]

    q_dst = qbuf.at[y, zslot, :, pl.ds(0, HD)]
    k_dst = kv.at[z, xh, 0, xl, c, :, pl.ds(0, HD)]
    v_dst = kv.at[z, xh, 1, xl, c, :, pl.ds(0, HD)]
    pltpu.make_async_copy(cols(q_ref, z), q_dst, q_got).start()
    pltpu.make_async_copy(cols(k_ref, z), k_dst, kv_got.at[z // GZ]).start()
    pltpu.make_async_copy(cols(v_ref, z), v_dst, kv_got.at[z // GZ]).start()

    def q_copy(i):
        h = far(i)
        return remote(cols(q_ref, h), q_dst, q_sent.at[i], q_got, dev(z2=h))

    def k_copy(i):
        h = far(i)
        return remote(cols(k_ref, h), k_dst, k_sent.at[i], kv_got.at[z // GZ], dev(z2=h))

    def v_copy(i):
        h = far(i)
        return remote(cols(v_ref, h), v_dst, v_sent.at[i], kv_got.at[z // GZ], dev(z2=h))

    def start_q(i, carry):
        q_copy(i).start()
        return carry

    def start_kv(i, carry):
        k_copy(i).start()
        v_copy(i).start()
        return carry

    lax.fori_loop(1, NZ, start_q, 0)
    lax.fori_loop(1, NZ, start_kv, 0)

    lane = lax.broadcasted_iota(jnp.int32, (4 * CH, HD), 1)

    def fill_kv(i, carry):
        zz, hh = i // 2, i % 2
        hot = jnp.where(lane == i, 1.0, 0.0).astype(BF16).reshape(2, 2, CH, HD)
        kv[zz, hh, 0, :, :, :, HD:] = hot
        kv[zz, hh, 1, :, :, :, HD:] = jnp.ones((2, 2, CH, HD), BF16)
        return carry

    lax.fori_loop(0, 2 * NZ, fill_kv, 0)
    for qt in range(4):
        for s in range(NZ):
            row = bias_ref[qt * NZ + s : qt * NZ + s + 1, :]
            qbuf[qt, s, :, HD:] = jnp.broadcast_to(row, (CH, HD)).astype(BF16)

    def zero(i, carry):
        qt, s = i // NZ, i % NZ
        acc[qt, s] = jnp.zeros((CH, 2 * HD), F32)
        top[qt, s] = jnp.full((CH, HD), -3e38, F32)
        return carry

    lax.fori_loop(0, 4 * NZ, zero, 0)

    q_slab = qbuf.at[y, :, :, pl.ds(0, HD)]
    wait_bytes(q_slab, q_got)
    y_copies = [
        remote(q_slab, q_slab, y_sent.at[dy - 1], y_got.at[dy - 1], dev(y2=(y + dy) % 4))
        for dy in range(1, 4)
    ]
    for copy in y_copies:
        copy.start()

    zq = z // GZ
    order = [zq, (zq + 1) % STEPS, (zq + 3) % STEPS, (zq + 2) % STEPS]

    def part(g, x2, c2=c):
        return kv.at[pl.ds(g * GZ, GZ), x2 // 2, :, x2 % 2, c2, :, pl.ds(0, HD)]

    x_copies = []

    def push(n, slot, g, x2, recv, device):
        ref = part(g, x2)
        copy = remote(ref, ref, x_sent.at[n, slot], recv, device)
        copy.start()
        x_copies.append(copy)

    sib = dev(c2=1 - c)

    def stage1(n):
        g = order[n]
        wait_bytes(part(g, x), kv_got.at[g])
        push(n, 0, g, x, x_got.at[n, 0], dev(x2=ahead))
        push(n, 1, g, x, x_got.at[n, 1], dev(x2=behind))
        push(n, 2, g, x, sib_got.at[n], sib)

    def stage2(n):
        g = order[n]
        wait_bytes(part(g, behind), x_got.at[n, 0])
        push(n, 3, g, behind, x_got.at[n, 2], dev(x2=ahead))
        push(n, 4, g, behind, sib_got.at[n], sib)
        wait_bytes(part(g, ahead), x_got.at[n, 1])
        push(n, 5, g, ahead, sib_got.at[n], sib)

    def stage3(n):
        g = order[n]
        wait_bytes(part(g, opposite), x_got.at[n, 2])
        push(n, 6, g, opposite, sib_got.at[n], sib)

    def stage4(n):
        g = order[n]
        wait_bytes(kv.at[pl.ds(g * GZ, GZ), :, :, :, 1 - c, :, pl.ds(0, HD)], sib_got.at[n])

    HB = NZ // 2
    ROWS = HB * CH

    def attend(n, qt, j):
        g = order[n]
        rows = pl.ds(j * HB, HB)
        qq = qbuf[qt, rows].reshape(ROWS, 2 * HD)
        kk = kv[pl.ds(g * GZ, GZ), :, 0].reshape(GZ * 8 * CH, 2 * HD)
        vv = kv[pl.ds(g * GZ, GZ), :, 1].reshape(GZ * 8 * CH, 2 * HD)
        s = lax.dot_general(qq, kk, (((1,), (1,)), ((), ())), preferred_element_type=F32)
        old = top[qt, rows].reshape(ROWS, HD)
        new = jnp.maximum(old, jnp.max(s, axis=1, keepdims=True))
        p = jnp.exp2((s - new[:, :1]) * SCALE).astype(BF16)
        pv = jnp.dot(p, vv, preferred_element_type=F32)
        fade = jnp.exp2((old - new) * SCALE)
        total = acc[qt, rows].reshape(ROWS, 2 * HD)
        total = jnp.concatenate([total[:, :HD] * fade, total[:, HD:] * fade], axis=1) + pv
        return total, new

    def attend_store(n, qt, j):
        total, new = attend(n, qt, j)
        acc[qt, pl.ds(j * HB, HB)] = total.reshape(HB, CH, 2 * HD)
        top[qt, pl.ds(j * HB, HB)] = new.reshape(HB, CH, HD)

    def blocks(n, lo, hi):
        def one(i, carry):
            attend_store(n, i // 2, i % 2)
            return carry

        lax.fori_loop(lo, hi, one, 0)

    stage1(0)
    stage2(0)
    stage3(0)
    for dy in range(1, 4):
        y_copies[dy - 1].wait_recv()
    stage4(0)
    for n in range(STEPS - 1):
        stage1(n + 1)
        blocks(n, 0, 4)
        stage2(n + 1)
        blocks(n, 4, 8)
        stage3(n + 1)
        stage4(n + 1)

    eye = (
        lax.broadcasted_iota(jnp.int32, (HD, HD), 0) == lax.broadcasted_iota(jnp.int32, (HD, HD), 1)
    )

    def o_copy(i):
        d, j = i // 2, i % 2
        return remote(
            osend.at[d, j], orecv.at[d, j], o_sent.at[d, j], o_got.at[d, j],
            dev(y2=(y + d + 1) % 4),
        )

    def l_copy(i):
        d, j = i // 2, i % 2
        return remote(
            lsend.at[d, j], lrecv.at[d, j], l_sent.at[d, j], l_got.at[d, j],
            dev(y2=(y + d + 1) % 4),
        )

    def finish(i):
        total, new = attend(STEPS - 1, (y + i // 2 + 1) % 4, i % 2)
        summed = total[:, HD:]
        return total[:, :HD] / summed, new * SCALE + jnp.log2(summed)

    def last(i, carry):
        o, lse = finish(i)
        d, j = i // 2, i % 2
        osend[d, j] = o.astype(BF16).reshape(HB, CH, HD)
        lsend[d, j] = jnp.sum(
            jnp.where(eye[None], lse.reshape(ROWS // HD, HD, HD), 0.0), axis=1
        )
        o_copy(i).start()
        l_copy(i).start()
        return carry

    lax.fori_loop(0, 6, last, 0)

    def last_own(j, carry):
        o, lse = finish(6 + j)
        oown[j] = o
        lown[j] = lse
        return carry

    lax.fori_loop(0, 2, last_own, 0)

    r_dst = cols(out_ref, z)

    def r_copy(j, i):
        z2 = 2 * i + j
        return remote(zsend.at[j, i], r_dst, r_sent.at[j, i], r_got, dev(z2=z2))

    def combine(j, carry):
        parts = [oown[j]]
        weights = [lown[j]]
        for d in range(3):
            o_copy(2 * d + j).wait_recv()
            l_copy(2 * d + j).wait_recv()
            stat = lrecv[d, j]
            wide = jnp.sum(
                jnp.where(eye[None], jnp.broadcast_to(stat[:, None, :], (ROWS // HD, HD, HD)), 0.0),
                axis=2, keepdims=True,
            )
            weights.append(jnp.broadcast_to(wide, (ROWS // HD, HD, HD)).reshape(ROWS, HD))
            parts.append(orecv[d, j].reshape(ROWS, HD).astype(F32))
        high = functools.reduce(jnp.maximum, weights)
        weights = [jnp.exp2(w - high) for w in weights]
        mixed = sum(w * o for w, o in zip(weights, parts)) / sum(weights)
        zsend[j] = mixed.astype(BF16).reshape(HB, CH, HD)

        def home(i, carry2):
            z2 = 2 * i + j

            @pl.when(z2 != z)
            def _():
                r_copy(j, i).start()

            @pl.when(z2 == z)
            def _():
                pltpu.make_async_copy(zsend.at[j, i], r_dst, r_got).start()

            return carry2

        lax.fori_loop(0, HB, home, 0)
        return carry

    lax.fori_loop(0, 2, combine, 0)
    wait_bytes(out_ref, r_got)

    def drain_z(i, carry):
        q_copy(i).wait_send()
        k_copy(i).wait_send()
        v_copy(i).wait_send()
        return carry

    lax.fori_loop(1, NZ, drain_z, 0)
    for copy in y_copies + x_copies:
        copy.wait_send()

    def drain_o(i, carry):
        o_copy(i).wait_send()
        l_copy(i).wait_send()
        return carry

    lax.fori_loop(0, 6, drain_o, 0)

    def drain_r(i, carry):
        @pl.when(i != z)
        def _():
            r_copy(i % 2, i // 2).wait_send()

        return carry

    lax.fori_loop(0, NZ, drain_r, 0)


def attention(queries, keys, values, bias):
    dma = pltpu.SemaphoreType.DMA
    vmem = pl.BlockSpec(memory_space=pltpu.VMEM)
    return pl.pallas_call(
        kernel,
        out_shape=jax.ShapeDtypeStruct(queries.shape, BF16),
        in_specs=[vmem] * 4,
        out_specs=vmem,
        scratch_shapes=[
            pltpu.VMEM((4, NZ, CH, 2 * HD), BF16),
            pltpu.VMEM((NZ, 2, 2, 2, 2, CH, 2 * HD), BF16),
            pltpu.VMEM((4, NZ, CH, 2 * HD), F32),
            pltpu.VMEM((4, NZ, CH, HD), F32),
            pltpu.VMEM((3, 2, NZ // 2, CH, HD), BF16),
            pltpu.VMEM((3, 2, 2, HD), F32),
            pltpu.VMEM((3, 2, NZ // 2, CH, HD), BF16),
            pltpu.VMEM((3, 2, 2, HD), F32),
            pltpu.VMEM((2, NZ // 2 * CH, HD), F32),
            pltpu.VMEM((2, NZ // 2 * CH, HD), F32),
            pltpu.VMEM((2, NZ // 2, CH, HD), BF16),
            dma((NZ,)), dma((NZ,)), dma((NZ,)),
            dma, dma((STEPS,)),
            dma((3,)), dma((3,)),
            dma((STEPS, 7)), dma((STEPS, 3)), dma((STEPS,)),
            dma((3, 2)), dma((3, 2)), dma((3, 2)), dma((3, 2)),
            dma((2, NZ // 2)), dma,
        ],
        compiler_params=pltpu.CompilerParams(
            collective_id=0, has_side_effects=True, vmem_limit_bytes=40 * 2**20
        ),
        name="attention",
    )(queries, keys, values, bias)


def per_device(queries, keys, values, tile_mask, frame_order):
    b, u = lax.axis_index("blk"), lax.axis_index("uly")
    xh, y = b % 2, u // 4
    order = frame_order.reshape(NZ, 2)
    mine = lax.dynamic_index_in_dim(order, xh, 1, keepdims=False)
    mine = jnp.transpose(mine.reshape(NZ // 2, 2)).reshape(NZ)
    columns = lax.dynamic_index_in_dim(tile_mask, y, 3, keepdims=False)
    chosen = columns[mine][:, frame_order]
    bias = jnp.where(jnp.transpose(chosen, (2, 0, 1)) > 0, 0.0, MASKED)
    bias = jnp.pad(bias.reshape(4 * NZ, 2 * NZ), ((0, 0), (0, HD - 2 * NZ)))
    return attention(queries, keys, values, bias)


def solution(mesh):
    rows = P(("blk", "uly"), None)
    return jax.shard_map(
        per_device,
        mesh=mesh,
        in_specs=(rows, rows, rows, P(), P()),
        out_specs=rows,
        check_vma=False,
    )
```

```python
import functools
import math

import jax
import jax.numpy as jnp
from jax import lax
from jax.experimental import pallas as pl
from jax.experimental.pallas import tpu as pltpu
from jax.sharding import PartitionSpec as P

HD = 128
CH = 32
NZ = 16
GZ = 4
STEPS = NZ // GZ
MASKED = -1e30
SCALE = math.log2(math.e) / math.sqrt(HD)
MESH = pl.DeviceIdType.MESH
F32 = jnp.float32
BF16 = jnp.bfloat16


def kernel(
    q_ref, k_ref, v_ref, mask_ref, order_ref, out_ref,
    mask, frames, qbuf, kv, acc, top, osend, lsend, orecv, lrecv, oown, lown, zsend,
    q_sent, k_sent, v_sent, q_got, kv_got, y_sent, y_got,
    x_sent, x_got, sib_got, o_sent, l_sent, o_got, l_got, r_sent, r_got, in_got,
):
    b, u = lax.axis_index("blk"), lax.axis_index("uly")
    z, xh = b // 2, b % 2
    y, xl, c = u // 4, (u // 2) % 2, u % 2
    x = xh * 2 + xl
    ahead, behind, opposite = (x + 1 + 2 * c) % 4, (x + 3 - 2 * c) % 4, (x + 2) % 4

    def dev(z2=z, x2=x, y2=y, c2=c):
        return {"blk": z2 * 2 + x2 // 2, "uly": y2 * 4 + (x2 % 2) * 2 + c2}

    def remote(src, dst, send, recv, device):
        return pltpu.make_async_remote_copy(
            src_ref=src, dst_ref=dst, send_sem=send, recv_sem=recv,
            device_id=device, device_id_type=MESH,
        )

    def wait_bytes(ref, sem):
        pltpu.make_async_copy(ref, ref, sem).wait()

    def plane(i):
        return lax.rem(z + NZ + (2 * (i % 2) - 1) * ((i + 1) // 2), NZ)

    barrier = pltpu.get_barrier_semaphore()
    partners = [dev(z2=plane(i)) for i in range(NZ - 1, 0, -1)]
    partners += [dev(y2=lax.rem(y + dy, 4)) for dy in (2, 1, 3)]
    partners += [dev(x2=ahead), dev(x2=behind), dev(c2=1 - c)]
    for partner in partners:
        pl.semaphore_signal(barrier, inc=1, device_id=partner, device_id_type=MESH)
    mask_copy = pltpu.make_async_copy(mask_ref, mask, in_got.at[0])
    frames_copy = pltpu.make_async_copy(order_ref, frames, in_got.at[1])
    mask_copy.start()
    frames_copy.start()
    pl.semaphore_wait(barrier, len(partners))

    zslot = (z % 2) * (NZ // 2) + z // 2

    def cols(ref, h):
        return ref.at[:, pl.ds(pl.multiple_of(h * HD, HD), HD)]

    q_dst = qbuf.at[y, zslot, :, pl.ds(0, HD)]
    k_dst = kv.at[z, xh, 0, xl, c, :, pl.ds(0, HD)]
    v_dst = kv.at[z, xh, 1, xl, c, :, pl.ds(0, HD)]
    pltpu.make_async_copy(cols(q_ref, z), q_dst, q_got).start()
    pltpu.make_async_copy(cols(k_ref, z), k_dst, kv_got.at[z // GZ]).start()
    pltpu.make_async_copy(cols(v_ref, z), v_dst, kv_got.at[z // GZ]).start()

    def q_copy(i):
        h = plane(i)
        return remote(cols(q_ref, h), q_dst, q_sent.at[i], q_got, dev(z2=h))

    def k_copy(i):
        h = plane(i)
        return remote(cols(k_ref, h), k_dst, k_sent.at[i], kv_got.at[z // GZ], dev(z2=h))

    def v_copy(i):
        h = plane(i)
        return remote(cols(v_ref, h), v_dst, v_sent.at[i], kv_got.at[z // GZ], dev(z2=h))

    def start_q(i, carry):
        q_copy(i).start()
        return carry

    def start_kv(i, carry):
        k_copy(i).start()
        v_copy(i).start()
        return carry

    lax.fori_loop(1, NZ, start_q, 0)
    lax.fori_loop(1, NZ, start_kv, 0)

    lane = lax.broadcasted_iota(jnp.int32, (4 * CH, HD), 1)
    mask_copy.wait()
    frames_copy.wait()

    def fill_kv(i, carry):
        zz, hh = i // 2, i % 2
        hot = jnp.where(lane == frames[i], 1.0, 0.0).astype(BF16).reshape(2, 2, CH, HD)
        kv[zz, hh, 0, :, :, :, HD:] = hot
        kv[zz, hh, 1, :, :, :, HD:] = jnp.ones((2, 2, CH, HD), BF16)
        return carry

    lax.fori_loop(0, 2 * NZ, fill_kv, 0)

    def fill_q(zz, carry):
        s = (zz % 2) * (NZ // 2) + zz // 2
        rows = mask[frames[2 * zz + xh], :, y, :]
        rows = jnp.where(rows > 0, 0.0, MASKED)
        for qt in range(4):
            qbuf[qt, s, :, HD:] = jnp.zeros((CH, HD), BF16)
            wide = jnp.broadcast_to(rows[qt : qt + 1], (CH, 2 * NZ)).astype(BF16)
            qbuf[qt, s, :, HD : HD + 2 * NZ] = wide
        return carry

    lax.fori_loop(0, NZ, fill_q, 0)

    def zero(i, carry):
        qt, s = i // NZ, i % NZ
        acc[qt, s] = jnp.zeros((CH, 2 * HD), F32)
        top[qt, s] = jnp.full((CH, HD), -3e38, F32)
        return carry

    lax.fori_loop(0, 4 * NZ, zero, 0)

    q_slab = qbuf.at[y, :, :, pl.ds(0, HD)]
    wait_bytes(q_slab, q_got)
    y_copies = [
        remote(q_slab, q_slab, y_sent.at[dy - 1], y_got.at[dy - 1], dev(y2=(y + dy) % 4))
        for dy in range(1, 4)
    ]
    for copy in y_copies:
        copy.start()

    zq = z // GZ

    def group(n):
        return lax.rem(zq + n + (n // 2) * (1 - 2 * (n % 2)), STEPS)

    def part(g, x2, c2=c):
        return kv.at[pl.ds(g * GZ, GZ), x2 // 2, :, x2 % 2, c2, :, pl.ds(0, HD)]

    def push(n, slot, x2, recv, device):
        ref = part(group(n), x2)
        return remote(ref, ref, x_sent.at[n, slot], recv, device)

    sib = dev(c2=1 - c)

    def pushes(n):
        return [
            push(n, 0, x, x_got.at[n, 0], dev(x2=ahead)),
            push(n, 1, x, x_got.at[n, 1], dev(x2=behind)),
            push(n, 2, x, sib_got.at[n], sib),
            push(n, 3, behind, x_got.at[n, 2], dev(x2=ahead)),
            push(n, 4, behind, sib_got.at[n], sib),
            push(n, 5, ahead, sib_got.at[n], sib),
            push(n, 6, opposite, sib_got.at[n], sib),
        ]

    def stage1(n):
        g = group(n)
        wait_bytes(part(g, x), kv_got.at[g])
        for copy in pushes(n)[:3]:
            copy.start()

    def stage2(n):
        g = group(n)
        wait_bytes(part(g, behind), x_got.at[n, 0])
        for copy in pushes(n)[3:5]:
            copy.start()
        wait_bytes(part(g, ahead), x_got.at[n, 1])
        pushes(n)[5].start()

    def stage3(n):
        g = group(n)
        wait_bytes(part(g, opposite), x_got.at[n, 2])
        pushes(n)[6].start()

    def stage4(n):
        g = group(n)
        wait_bytes(kv.at[pl.ds(g * GZ, GZ), :, :, :, 1 - c, :, pl.ds(0, HD)], sib_got.at[n])

    HB = NZ // 2
    ROWS = HB * CH

    def attend(n, qt, j):
        g = group(n)
        rows = pl.ds(j * HB, HB)
        qq = qbuf[qt, rows].reshape(ROWS, 2 * HD)
        kk = kv[pl.ds(g * GZ, GZ), :, 0].reshape(GZ * 8 * CH, 2 * HD)
        vv = kv[pl.ds(g * GZ, GZ), :, 1].reshape(GZ * 8 * CH, 2 * HD)
        s = lax.dot_general(qq, kk, (((1,), (1,)), ((), ())), preferred_element_type=F32)
        old = top[qt, rows].reshape(ROWS, HD)
        new = jnp.maximum(old, jnp.max(s, axis=1, keepdims=True))
        p = jnp.exp2((s - new[:, :1]) * SCALE).astype(BF16)
        pv = jnp.dot(p, vv, preferred_element_type=F32)
        fade = jnp.exp2((old - new) * SCALE)
        total = acc[qt, rows].reshape(ROWS, 2 * HD)
        total = jnp.concatenate([total[:, :HD] * fade, total[:, HD:] * fade], axis=1) + pv
        return total, new

    def attend_store(n, qt, j):
        total, new = attend(n, qt, j)
        acc[qt, pl.ds(j * HB, HB)] = total.reshape(HB, CH, 2 * HD)
        top[qt, pl.ds(j * HB, HB)] = new.reshape(HB, CH, HD)

    stage1(0)
    stage2(0)
    stage3(0)
    for dy in range(1, 4):
        y_copies[dy - 1].wait_recv()
    stage4(0)

    def step(n, carry):
        stage1(n + 1)
        for qt in range(4):
            attend_store(n, qt, 0)
        stage2(n + 1)
        for qt in range(4):
            attend_store(n, qt, 1)
        stage3(n + 1)
        stage4(n + 1)
        return carry

    lax.fori_loop(0, STEPS - 1, step, 0)

    eye = (
        lax.broadcasted_iota(jnp.int32, (HD, HD), 0) == lax.broadcasted_iota(jnp.int32, (HD, HD), 1)
    )

    def o_copy(d, j):
        return remote(
            osend.at[d, j], orecv.at[d, j], o_sent.at[d, j], o_got.at[d, j],
            dev(y2=lax.rem(y + d + 1, 4)),
        )

    def l_copy(d, j):
        return remote(
            lsend.at[d, j], lrecv.at[d, j], l_sent.at[d, j], l_got.at[d, j],
            dev(y2=lax.rem(y + d + 1, 4)),
        )

    def last(j, carry):
        for d in (1, 0, 2, 3):
            total, new = attend(STEPS - 1, lax.rem(y + d + 1, 4), j)
            summed = total[:, HD:]
            o = total[:, :HD] / summed
            lse = new * SCALE + jnp.log2(summed)
            if d == 3:
                oown[j] = o
                lown[j] = lse
            else:
                osend[d, j] = o.astype(BF16).reshape(HB, CH, HD)
                lsend[d, j] = jnp.sum(
                    jnp.where(eye[None], lse.reshape(ROWS // HD, HD, HD), 0.0), axis=1
                )
        for d in (1, 0, 2):
            o_copy(d, j).start()
            l_copy(d, j).start()
        return carry

    lax.fori_loop(0, 2, last, 0)

    r_dst = cols(out_ref, z)

    def r_copy(j, i):
        z2 = 2 * i + j
        return remote(zsend.at[j, i], r_dst, r_sent.at[j, i], r_got, dev(z2=z2))

    def combine(j, carry):
        parts = [oown[j]]
        weights = [lown[j]]
        for d in range(3):
            o_copy(d, j).wait_recv()
            l_copy(d, j).wait_recv()
            stat = lrecv[d, j]
            wide = jnp.sum(
                jnp.where(eye[None], jnp.broadcast_to(stat[:, None, :], (ROWS // HD, HD, HD)), 0.0),
                axis=2, keepdims=True,
            )
            weights.append(jnp.broadcast_to(wide, (ROWS // HD, HD, HD)).reshape(ROWS, HD))
            parts.append(orecv[d, j].reshape(ROWS, HD).astype(F32))
        high = functools.reduce(jnp.maximum, weights)
        weights = [jnp.exp2(w - high) for w in weights]
        mixed = sum(w * o for w, o in zip(weights, parts)) / sum(weights)
        zsend[j] = mixed.astype(BF16).reshape(HB, CH, HD)

        def home(i, carry2):
            z2 = 2 * i + j

            @pl.when(z2 != z)
            def _():
                r_copy(j, i).start()

            @pl.when(z2 == z)
            def _():
                pltpu.make_async_copy(zsend.at[j, i], r_dst, r_got).start()

            return carry2

        lax.fori_loop(0, HB, home, 0)
        return carry

    lax.fori_loop(0, 2, combine, 0)
    wait_bytes(out_ref, r_got)

    def drain_z(i, carry):
        q_copy(i).wait_send()
        k_copy(i).wait_send()
        v_copy(i).wait_send()
        return carry

    lax.fori_loop(1, NZ, drain_z, 0)
    for copy in y_copies:
        copy.wait_send()

    def drain_x(n, carry):
        for copy in pushes(n):
            copy.wait_send()
        return carry

    lax.fori_loop(0, STEPS, drain_x, 0)

    def drain_o(j, carry):
        for d in range(3):
            o_copy(d, j).wait_send()
            l_copy(d, j).wait_send()
        return carry

    lax.fori_loop(0, 2, drain_o, 0)

    def drain_r(i, carry):
        @pl.when(i != z)
        def _():
            r_copy(i % 2, i // 2).wait_send()

        return carry

    lax.fori_loop(0, NZ, drain_r, 0)


def attention(queries, keys, values, tile_mask, frame_order):
    dma = pltpu.SemaphoreType.DMA
    hbm = pl.BlockSpec(memory_space=pl.ANY)
    return pl.pallas_call(
        kernel,
        out_shape=jax.ShapeDtypeStruct(queries.shape, BF16),
        in_specs=[hbm] * 5,
        out_specs=hbm,
        scratch_shapes=[
            pltpu.VMEM((2 * NZ, 4, 4, 2 * NZ), jnp.int32),
            pltpu.SMEM((2 * NZ,), jnp.int32),
            pltpu.VMEM((4, NZ, CH, 2 * HD), BF16),
            pltpu.VMEM((NZ, 2, 2, 2, 2, CH, 2 * HD), BF16),
            pltpu.VMEM((4, NZ, CH, 2 * HD), F32),
            pltpu.VMEM((4, NZ, CH, HD), F32),
            pltpu.VMEM((3, 2, NZ // 2, CH, HD), BF16),
            pltpu.VMEM((3, 2, 2, HD), F32),
            pltpu.VMEM((3, 2, NZ // 2, CH, HD), BF16),
            pltpu.VMEM((3, 2, 2, HD), F32),
            pltpu.VMEM((2, NZ // 2 * CH, HD), F32),
            pltpu.VMEM((2, NZ // 2 * CH, HD), F32),
            pltpu.VMEM((2, NZ // 2, CH, HD), BF16),
            dma((NZ,)), dma((NZ,)), dma((NZ,)),
            dma, dma((STEPS,)),
            dma((3,)), dma((3,)),
            dma((STEPS, 7)), dma((STEPS, 3)), dma((STEPS,)),
            dma((3, 2)), dma((3, 2)), dma((3, 2)), dma((3, 2)),
            dma((2, NZ // 2)), dma, dma((2,)),
        ],
        compiler_params=pltpu.CompilerParams(
            collective_id=0, has_side_effects=True, vmem_limit_bytes=56 * 2**20
        ),
        name="attention",
    )(queries, keys, values, tile_mask, frame_order)


def per_device(queries, keys, values, tile_mask, frame_order):
    by_key = jnp.transpose(tile_mask, (0, 2, 3, 1))
    return attention(queries, keys, values, by_key, frame_order)


def solution(mesh):
    rows = P(("blk", "uly"), None)
    return jax.shard_map(
        per_device,
        mesh=mesh,
        in_specs=(rows, rows, rows, P(), P()),
        out_specs=rows,
        check_vma=False,
    )
```

```python
import functools
import math

import jax
import jax.numpy as jnp
from jax import lax
from jax.experimental import pallas as pl
from jax.experimental.pallas import tpu as pltpu
from jax.sharding import PartitionSpec as P

HD = 128
CH = 32
NZ = 16
GZ = 4
STEPS = NZ // GZ
GROUPS = ((0, 4), (4, 4), (8, 4), (12, 2), (14, 2))
KSTEPS = len(GROUPS)
MASKED = -1e30
SCALE = math.log2(math.e) / math.sqrt(HD)
MESH = pl.DeviceIdType.MESH
F32 = jnp.float32
BF16 = jnp.bfloat16


def kernel(
    q_ref, k_ref, v_ref, mask_ref, order_ref, out_ref,
    mask, frames, qbuf, kv, acc, top, osend, lsend, orecv, lrecv, oown, lown, zsend,
    q_sent, k_sent, v_sent, q_got, kv_got, y_sent, y_got,
    x_sent, x_got, other_got, o_sent, l_sent, o_got, l_got, r_sent, r_got, in_got,
):
    b, u = lax.axis_index("blk"), lax.axis_index("uly")
    z, xh = b // 2, b % 2
    y, xl, c = u // 4, (u // 2) % 2, u % 2
    x = xh * 2 + xl
    kpos, qpos = x * (1 - c) + y * c, y * (1 - c) + x * c

    def dev(z2=z, x2=x, y2=y, c2=c):
        return {"blk": z2 * 2 + x2 // 2, "uly": y2 * 4 + (x2 % 2) * 2 + c2}

    def on_key_axis(core, d, c2):
        x2, y2 = lax.rem(x + d * (1 - core), 4), lax.rem(y + d * core, 4)
        return dev(x2=x2, y2=y2, c2=c2)

    def remote(src, dst, send, recv, device):
        return pltpu.make_async_remote_copy(
            src_ref=src, dst_ref=dst, send_sem=send, recv_sem=recv,
            device_id=device, device_id_type=MESH,
        )

    def wait_bytes(ref, sem):
        pltpu.make_async_copy(ref, ref, sem).wait()

    def offset(t):
        return (2 * (t % 2) - 1) * ((t + 1) // 2)

    def source(t):
        return lax.rem(z + NZ + offset(t), NZ)

    def target(t):
        return lax.rem(z + NZ - offset(t), NZ)

    barrier = pltpu.get_barrier_semaphore()
    partners = [dev(z2=target(i)) for i in range(NZ - 1, 0, -1)]
    partners += [dev(y2=lax.rem(y + dy, 4)) for dy in (2, 1, 3)]
    partners += [dev(x2=lax.rem(x + dx, 4)) for dx in (2, 1, 3)]
    partners += [dev(y2=lax.rem(y + dy, 4), c2=1 - c) for dy in (2, 1, 3)]
    partners += [dev(x2=lax.rem(x + dx, 4), c2=1 - c) for dx in (2, 1, 3, 0)]
    for partner in partners:
        pl.semaphore_signal(barrier, inc=1, device_id=partner, device_id_type=MESH)
    mask_copy = pltpu.make_async_copy(mask_ref, mask, in_got.at[0])
    frames_copy = pltpu.make_async_copy(order_ref, frames, in_got.at[1])
    mask_copy.start()
    frames_copy.start()
    pl.semaphore_wait(barrier, len(partners))

    def cols(ref, h):
        return ref.at[:, pl.ds(pl.multiple_of(h * HD, HD), HD)]

    def q_dst(t):
        return qbuf.at[qpos, t, :, pl.ds(0, HD)]

    def kv_dst(t, which):
        return kv.at[t, kpos, which, c, :, pl.ds(0, HD)]

    pltpu.make_async_copy(cols(q_ref, z), q_dst(0), q_got.at[0]).start()
    pltpu.make_async_copy(cols(k_ref, z), kv_dst(0, 0), kv_got.at[0]).start()
    pltpu.make_async_copy(cols(v_ref, z), kv_dst(0, 1), kv_got.at[0]).start()

    def q_copy(t):
        h = target(t)
        return remote(cols(q_ref, h), q_dst(t), q_sent.at[t], q_got.at[t // GZ], dev(z2=h))

    def k_copy(t):
        h = target(t)
        return remote(cols(k_ref, h), kv_dst(t, 0), k_sent.at[t], kv_got.at[t // 4 + t // 14], dev(z2=h))

    def v_copy(t):
        h = target(t)
        return remote(cols(v_ref, h), kv_dst(t, 1), v_sent.at[t], kv_got.at[t // 4 + t // 14], dev(z2=h))

    def start_q(t, carry):
        q_copy(t).start()
        return carry

    def start_kv(t, carry):
        k_copy(t).start()
        v_copy(t).start()
        return carry

    def sent_q(t, carry):
        q_copy(t).wait_send()
        return carry

    def sent_kv(t, carry):
        k_copy(t).wait_send()
        v_copy(t).wait_send()
        return carry

    lax.fori_loop(1, NZ, lambda i, carry: start_q(NZ - i, carry), 0)
    lax.fori_loop(1, NZ, start_kv, 0)

    lane = lax.broadcasted_iota(jnp.int32, (2 * CH, HD), 1)
    mask_copy.wait()
    frames_copy.wait()

    def fill(i, carry):
        t, a = i // 4, i % 4
        first = 2 * source(t)
        key_frame = frames[first + (a // 2) * (1 - c) + xh * c]
        key_tile = y * (1 - c) + a * c
        hot = jnp.where(lane == key_tile * 2 * NZ + key_frame, 1.0, 0.0).astype(BF16)
        kv[t, a, 0, :, :, HD:] = hot.reshape(2, CH, HD)
        kv[t, a, 1, :, :, HD:] = jnp.ones((2, CH, HD), BF16)
        query_frame = frames[first + xh * (1 - c) + (a // 2) * c]
        query_tile = a * (1 - c) + y * c
        rows = jnp.where(mask[query_frame, query_tile] > 0, 0.0, MASKED)
        row = jnp.concatenate([rows[kt : kt + 1] for kt in range(4)], axis=1)
        qbuf[a, t, :, HD:] = jnp.broadcast_to(row, (CH, HD)).astype(BF16)
        return carry

    lax.fori_loop(0, 4 * NZ, fill, 0)

    def zero(i, carry):
        qt, s = i // NZ, i % NZ
        acc[qt, s] = jnp.zeros((CH, 2 * HD), F32)
        top[qt, s] = jnp.full((CH, HD), -3e38, F32)
        return carry

    lax.fori_loop(0, 4 * NZ, zero, 0)

    def q_part(n):
        return qbuf.at[qpos, pl.ds(n * GZ, GZ), :, pl.ds(0, HD)]

    def y_copy(n, dy):
        there = on_key_axis(1 - c, dy, c)
        return remote(q_part(n), q_part(n), y_sent.at[n, dy], y_got.at[n, dy], there)

    for n in range(STEPS):
        wait_bytes(q_part(n), q_got.at[n])
        for dy in (2, 1, 3):
            y_copy(n, dy).start()

    def slots(n):
        return pl.ds(*GROUPS[n])

    def part(n, a):
        return kv.at[slots(n), a, :, c, :, pl.ds(0, HD)]

    def across(n):
        own, there = part(n, kpos), part(n, qpos)
        copies = []
        for d in (2, 1, 3):
            device = on_key_axis(c, d, c)
            copies.append(remote(own, own, x_sent.at[n, d], x_got.at[n, d], device))
            device = on_key_axis(1 - c, d, 1 - c)
            copies.append(remote(own, there, x_sent.at[n, 4 + d], other_got.at[n], device))
        copies.append(remote(own, there, x_sent.at[n, 4], other_got.at[n], dev(c2=1 - c)))
        return copies

    def stage1(n):
        wait_bytes(part(n, kpos), kv_got.at[n])
        for copy in across(n):
            copy.start()

    def stage2(n):
        for d in (1, 3, 2):
            wait_bytes(part(n, lax.rem(kpos + 4 - d, 4)), x_got.at[n, d])
        wait_bytes(kv.at[slots(n), :, :, 1 - c, :, pl.ds(0, HD)], other_got.at[n])

    HB = NZ // 2
    ROWS = HB * CH

    def attend(n, qt, j):
        rows = pl.ds(j * HB, HB)
        qq = qbuf[qt, rows].reshape(ROWS, 2 * HD)
        kk = kv[slots(n), :, 0].reshape(GROUPS[n][1] * 8 * CH, 2 * HD)
        vv = kv[slots(n), :, 1].reshape(GROUPS[n][1] * 8 * CH, 2 * HD)
        s = lax.dot_general(qq, kk, (((1,), (1,)), ((), ())), preferred_element_type=F32)
        old = top[qt, rows].reshape(ROWS, HD)
        new = jnp.maximum(old, jnp.max(s, axis=1, keepdims=True))
        p = jnp.exp2((s - new[:, :1]) * SCALE).astype(BF16)
        pv = jnp.dot(p, vv, preferred_element_type=F32)
        fade = jnp.exp2((old - new) * SCALE)
        total = acc[qt, rows].reshape(ROWS, 2 * HD)
        total = jnp.concatenate([total[:, :HD] * fade, total[:, HD:] * fade], axis=1) + pv
        return total, new

    def attend_store(n, qt, j):
        total, new = attend(n, qt, j)
        acc[qt, pl.ds(j * HB, HB)] = total.reshape(HB, CH, 2 * HD)
        top[qt, pl.ds(j * HB, HB)] = new.reshape(HB, CH, HD)

    stage1(0)
    stage1(1)
    for n in range(STEPS):
        for dy in (2, 1, 3):
            y_copy(n, dy).wait_recv()
    stage2(0)

    def half(n, j):
        for qt in range(4):
            attend_store(n, qt, j)

    half(0, 0)
    stage2(1)
    half(0, 1)
    stage1(2)
    half(1, 0)
    stage1(3)
    half(1, 1)
    stage2(2)
    stage1(4)
    half(2, 0)
    stage2(3)
    half(2, 1)
    half(3, 0)
    half(3, 1)
    stage2(4)

    eye = (
        lax.broadcasted_iota(jnp.int32, (HD, HD), 0) == lax.broadcasted_iota(jnp.int32, (HD, HD), 1)
    )

    def o_copy(d, j):
        return remote(
            osend.at[d, j], orecv.at[d, j], o_sent.at[d, j], o_got.at[d, j],
            on_key_axis(1 - c, d + 1, c),
        )

    def l_copy(d, j):
        return remote(
            lsend.at[d, j], lrecv.at[d, j], l_sent.at[d, j], l_got.at[d, j],
            on_key_axis(1 - c, d + 1, c),
        )

    def last(j, carry):
        for d in (1, 0, 2, 3):
            total, new = attend(KSTEPS - 1, lax.rem(qpos + d + 1, 4), j)
            summed = total[:, HD:]
            o = total[:, :HD] / summed
            lse = new * SCALE + jnp.log2(summed)
            if d == 3:
                oown[j] = o
                lown[j] = lse
            else:
                osend[d, j] = o.astype(BF16).reshape(HB, CH, HD)
                lsend[d, j] = jnp.sum(
                    jnp.where(eye[None], lse.reshape(ROWS // HD, HD, HD), 0.0), axis=1
                )
                o_copy(d, j).start()
                l_copy(d, j).start()
        return carry

    lax.fori_loop(0, 2, lambda i, carry: last(1 - i, carry), 0)

    r_dst = cols(out_ref, z)

    def r_copy(j, i):
        z2 = source(j * HB + i)
        return remote(zsend.at[j, i], r_dst, r_sent.at[j, i], r_got, dev(z2=z2))

    def combine(j, carry):
        parts = [oown[j]]
        weights = [lown[j]]
        for d in range(3):
            o_copy(d, j).wait_recv()
            l_copy(d, j).wait_recv()
            stat = lrecv[d, j]
            wide = jnp.sum(
                jnp.where(eye[None], jnp.broadcast_to(stat[:, None, :], (ROWS // HD, HD, HD)), 0.0),
                axis=2, keepdims=True,
            )
            weights.append(jnp.broadcast_to(wide, (ROWS // HD, HD, HD)).reshape(ROWS, HD))
            parts.append(orecv[d, j].reshape(ROWS, HD).astype(F32))
        high = functools.reduce(jnp.maximum, weights)
        weights = [jnp.exp2(w - high) for w in weights]
        mixed = sum(w * o for w, o in zip(weights, parts)) / sum(weights)
        zsend[j] = mixed.astype(BF16).reshape(HB, CH, HD)

        def home(i, carry2):
            r_copy(j, i).start()
            return carry2

        lax.fori_loop(1 - j, HB, home, 0)
        return carry

    combine(1, 0)
    combine(0, 0)
    pltpu.make_async_copy(zsend.at[0, 0], r_dst, r_got).start()
    wait_bytes(out_ref, r_got)

    lax.fori_loop(1, NZ, sent_q, 0)
    lax.fori_loop(1, NZ, sent_kv, 0)
    def drain_y(n, carry):
        for dy in (2, 1, 3):
            y_copy(n, dy).wait_send()
        return carry

    lax.fori_loop(0, STEPS, drain_y, 0)

    for n in range(KSTEPS):
        for copy in across(n):
            copy.wait_send()

    def drain_o(j, carry):
        for d in range(3):
            o_copy(d, j).wait_send()
            l_copy(d, j).wait_send()
        return carry

    lax.fori_loop(0, 2, drain_o, 0)

    def drain_r(i, carry):
        r_copy(i // HB, i % HB).wait_send()
        return carry

    lax.fori_loop(1, NZ, drain_r, 0)


def attention(queries, keys, values, tile_mask, frame_order):
    dma = pltpu.SemaphoreType.DMA
    hbm = pl.BlockSpec(memory_space=pl.ANY)
    return pl.pallas_call(
        kernel,
        out_shape=jax.ShapeDtypeStruct(queries.shape, BF16),
        in_specs=[hbm] * 5,
        out_specs=hbm,
        scratch_shapes=[
            pltpu.VMEM((2 * NZ, 4, 4, 2 * NZ), jnp.int32),
            pltpu.SMEM((2 * NZ,), jnp.int32),
            pltpu.VMEM((4, NZ, CH, 2 * HD), BF16),
            pltpu.VMEM((NZ, 4, 2, 2, CH, 2 * HD), BF16),
            pltpu.VMEM((4, NZ, CH, 2 * HD), F32),
            pltpu.VMEM((4, NZ, CH, HD), F32),
            pltpu.VMEM((3, 2, NZ // 2, CH, HD), BF16),
            pltpu.VMEM((3, 2, 2, HD), F32),
            pltpu.VMEM((3, 2, NZ // 2, CH, HD), BF16),
            pltpu.VMEM((3, 2, 2, HD), F32),
            pltpu.VMEM((2, NZ // 2 * CH, HD), F32),
            pltpu.VMEM((2, NZ // 2 * CH, HD), F32),
            pltpu.VMEM((2, NZ // 2, CH, HD), BF16),
            dma((NZ,)), dma((NZ,)), dma((NZ,)),
            dma((STEPS,)), dma((KSTEPS,)),
            dma((STEPS, 4)), dma((STEPS, 4)),
            dma((KSTEPS, 8)), dma((KSTEPS, 4)), dma((KSTEPS,)),
            dma((3, 2)), dma((3, 2)), dma((3, 2)), dma((3, 2)),
            dma((2, NZ // 2)), dma, dma((2,)),
        ],
        compiler_params=pltpu.CompilerParams(
            collective_id=0, has_side_effects=True, vmem_limit_bytes=56 * 2**20
        ),
        name="attention",
    )(queries, keys, values, tile_mask, frame_order)


def per_device(queries, keys, values, tile_mask, frame_order):
    by_key = jnp.transpose(tile_mask, (0, 2, 3, 1))
    return attention(queries, keys, values, by_key, frame_order)


def solution(mesh):
    rows = P(("blk", "uly"), None)
    return jax.shard_map(
        per_device,
        mesh=mesh,
        in_specs=(rows, rows, rows, P(), P()),
        out_specs=rows,
        check_vma=False,
    )
```

```python
import functools
import math

import jax
import jax.numpy as jnp
from jax import lax
from jax.experimental import pallas as pl
from jax.experimental.pallas import tpu as pltpu
from jax.sharding import PartitionSpec as P

HD = 128
CH = 32
NZ = 16
GZ = 4
STEPS = NZ // GZ
GROUPS = ((0, 2), (2, 4), (6, 4), (10, 2), (12, 2), (14, 2))
KSTEPS = len(GROUPS)
MASKED = -1e30
SCALE = math.log2(math.e) / math.sqrt(HD)
MESH = pl.DeviceIdType.MESH
F32 = jnp.float32
BF16 = jnp.bfloat16


def kernel(
    q_ref, k_ref, v_ref, mask_ref, order_ref, out_ref,
    mask, frames, qbuf, kv, acc, top, osend, lsend, orecv, lrecv, oown, lown, zsend,
    q_sent, k_sent, v_sent, q_got, kv_got, y_sent, y_got,
    x_sent, x_got, other_got, o_sent, l_sent, o_got, l_got, r_sent, r_got, in_got,
):
    b, u = lax.axis_index("blk"), lax.axis_index("uly")
    z, xh = b // 2, b % 2
    y, xl, c = u // 4, (u // 2) % 2, u % 2
    x = xh * 2 + xl
    kpos, qpos = x * (1 - c) + y * c, y * (1 - c) + x * c

    def dev(z2=z, x2=x, y2=y, c2=c):
        return {"blk": z2 * 2 + x2 // 2, "uly": y2 * 4 + (x2 % 2) * 2 + c2}

    def on_key_axis(core, d, c2):
        x2, y2 = lax.rem(x + d * (1 - core), 4), lax.rem(y + d * core, 4)
        return dev(x2=x2, y2=y2, c2=c2)

    def remote(src, dst, send, recv, device):
        return pltpu.make_async_remote_copy(
            src_ref=src, dst_ref=dst, send_sem=send, recv_sem=recv,
            device_id=device, device_id_type=MESH,
        )

    def wait_bytes(ref, sem):
        pltpu.make_async_copy(ref, ref, sem).wait()

    def offset(t):
        return (2 * (t % 2) - 1) * ((t + 1) // 2)

    def source(t):
        return lax.rem(z + NZ + offset(t), NZ)

    def target(t):
        return lax.rem(z + NZ - offset(t), NZ)

    barrier = pltpu.get_barrier_semaphore()
    partners = [dev(z2=target(i)) for i in range(NZ - 1, 0, -1)]
    partners += [dev(y2=lax.rem(y + dy, 4)) for dy in (2, 1, 3)]
    partners += [dev(x2=lax.rem(x + dx, 4)) for dx in (2, 1, 3)]
    partners += [dev(y2=lax.rem(y + dy, 4), c2=1 - c) for dy in (2, 1, 3)]
    partners += [dev(x2=lax.rem(x + dx, 4), c2=1 - c) for dx in (2, 1, 3, 0)]
    for partner in partners:
        pl.semaphore_signal(barrier, inc=1, device_id=partner, device_id_type=MESH)
    mask_copy = pltpu.make_async_copy(mask_ref, mask, in_got.at[0])
    frames_copy = pltpu.make_async_copy(order_ref, frames, in_got.at[1])
    mask_copy.start()
    frames_copy.start()
    pl.semaphore_wait(barrier, len(partners))

    def cols(ref, h):
        return ref.at[:, pl.ds(pl.multiple_of(h * HD, HD), HD)]

    def q_dst(t):
        return qbuf.at[qpos, t, :, pl.ds(0, HD)]

    def kv_dst(t, which):
        return kv.at[t, kpos, which, c, :, pl.ds(0, HD)]

    pltpu.make_async_copy(cols(q_ref, z), q_dst(0), q_got.at[0]).start()
    pltpu.make_async_copy(cols(k_ref, z), kv_dst(0, 0), kv_got.at[0]).start()
    pltpu.make_async_copy(cols(v_ref, z), kv_dst(0, 1), kv_got.at[0]).start()

    def q_copy(t):
        h = target(t)
        return remote(cols(q_ref, h), q_dst(t), q_sent.at[t], q_got.at[t // GZ], dev(z2=h))

    def k_copy(t):
        h = target(t)
        return remote(cols(k_ref, h), kv_dst(t, 0), k_sent.at[t], kv_got.at[(t + 2) // 4 + t // 12], dev(z2=h))

    def v_copy(t):
        h = target(t)
        return remote(cols(v_ref, h), kv_dst(t, 1), v_sent.at[t], kv_got.at[(t + 2) // 4 + t // 12], dev(z2=h))

    def start_q(t, carry):
        q_copy(t).start()
        return carry

    def start_kv(t, carry):
        k_copy(t).start()
        v_copy(t).start()
        return carry

    def sent_q(t, carry):
        q_copy(t).wait_send()
        return carry

    def sent_kv(t, carry):
        k_copy(t).wait_send()
        v_copy(t).wait_send()
        return carry

    lax.fori_loop(1, NZ, lambda i, carry: start_q(NZ - i, carry), 0)
    lax.fori_loop(1, NZ, start_kv, 0)

    lane = lax.broadcasted_iota(jnp.int32, (2 * CH, HD), 1)
    mask_copy.wait()
    frames_copy.wait()

    def fill(i, carry):
        t, a = i // 4, i % 4
        first = 2 * source(t)
        key_frame = frames[first + (a // 2) * (1 - c) + xh * c]
        key_tile = y * (1 - c) + a * c
        hot = jnp.where(lane == key_tile * 2 * NZ + key_frame, 1.0, 0.0).astype(BF16)
        kv[t, a, 0, :, :, HD:] = hot.reshape(2, CH, HD)
        kv[t, a, 1, :, :, HD:] = jnp.ones((2, CH, HD), BF16)
        query_frame = frames[first + xh * (1 - c) + (a // 2) * c]
        query_tile = a * (1 - c) + y * c
        rows = jnp.where(mask[query_frame, query_tile] > 0, 0.0, MASKED)
        row = jnp.concatenate([rows[kt : kt + 1] for kt in range(4)], axis=1)
        qbuf[a, t, :, HD:] = jnp.broadcast_to(row, (CH, HD)).astype(BF16)
        return carry

    lax.fori_loop(0, 4 * NZ, fill, 0)

    def zero(i, carry):
        qt, s = i // NZ, i % NZ
        acc[qt, s] = jnp.zeros((CH, 2 * HD), F32)
        top[qt, s] = jnp.full((CH, HD), -3e38, F32)
        return carry

    lax.fori_loop(0, 4 * NZ, zero, 0)

    def q_part(n):
        return qbuf.at[qpos, pl.ds(n * GZ, GZ), :, pl.ds(0, HD)]

    def y_copy(n, dy):
        there = on_key_axis(1 - c, dy, c)
        return remote(q_part(n), q_part(n), y_sent.at[n, dy], y_got.at[n, dy], there)

    for n in range(STEPS):
        wait_bytes(q_part(n), q_got.at[n])
        for dy in (2, 1, 3):
            y_copy(n, dy).start()

    def slots(n):
        return pl.ds(*GROUPS[n])

    def part(n, a):
        return kv.at[slots(n), a, :, c, :, pl.ds(0, HD)]

    def across(n):
        own, there = part(n, kpos), part(n, qpos)
        copies = []
        for d in (2, 1, 3):
            device = on_key_axis(c, d, c)
            copies.append(remote(own, own, x_sent.at[n, d], x_got.at[n, d], device))
            device = on_key_axis(1 - c, d, 1 - c)
            copies.append(remote(own, there, x_sent.at[n, 4 + d], other_got.at[n], device))
        copies.append(remote(own, there, x_sent.at[n, 4], other_got.at[n], dev(c2=1 - c)))
        return copies

    def stage1(n):
        wait_bytes(part(n, kpos), kv_got.at[n])
        for copy in across(n):
            copy.start()

    def stage2(n):
        for d in (1, 3, 2):
            wait_bytes(part(n, lax.rem(kpos + 4 - d, 4)), x_got.at[n, d])
        wait_bytes(kv.at[slots(n), :, :, 1 - c, :, pl.ds(0, HD)], other_got.at[n])

    HB = NZ // 2
    ROWS = HB * CH

    def attend(n, qt, j):
        rows = pl.ds(j * HB, HB)
        qq = qbuf[qt, rows].reshape(ROWS, 2 * HD)
        kk = kv[slots(n), :, 0].reshape(GROUPS[n][1] * 8 * CH, 2 * HD)
        vv = kv[slots(n), :, 1].reshape(GROUPS[n][1] * 8 * CH, 2 * HD)
        s = lax.dot_general(qq, kk, (((1,), (1,)), ((), ())), preferred_element_type=F32)
        old = top[qt, rows].reshape(ROWS, HD)
        new = jnp.maximum(old, jnp.max(s, axis=1, keepdims=True))
        p = jnp.exp2((s - new[:, :1]) * SCALE).astype(BF16)
        pv = jnp.dot(p, vv, preferred_element_type=F32)
        fade = jnp.exp2((old - new) * SCALE)
        total = acc[qt, rows].reshape(ROWS, 2 * HD)
        total = jnp.concatenate([total[:, :HD] * fade, total[:, HD:] * fade], axis=1) + pv
        return total, new

    def attend_store(n, qt, j):
        total, new = attend(n, qt, j)
        acc[qt, pl.ds(j * HB, HB)] = total.reshape(HB, CH, 2 * HD)
        top[qt, pl.ds(j * HB, HB)] = new.reshape(HB, CH, HD)

    stage1(0)
    stage1(1)
    for n in range(STEPS):
        for dy in (2, 1, 3):
            y_copy(n, dy).wait_recv()
    stage2(0)

    def half(n, j):
        for qt in range(4):
            attend_store(n, qt, j)

    def both(n):
        def one(j, carry):
            half(n, j)
            return carry

        lax.fori_loop(0, 2, one, 0)

    half(0, 0)
    half(0, 1)
    stage1(2)
    stage2(1)
    half(1, 0)
    half(1, 1)
    stage1(3)
    stage2(2)
    stage1(4)
    half(2, 0)
    half(2, 1)
    stage2(3)
    stage1(5)
    half(3, 0)
    half(3, 1)
    stage2(4)
    half(4, 0)
    half(4, 1)
    stage2(5)

    eye = (
        lax.broadcasted_iota(jnp.int32, (HD, HD), 0) == lax.broadcasted_iota(jnp.int32, (HD, HD), 1)
    )

    def o_copy(d, j):
        return remote(
            osend.at[d, j], orecv.at[d, j], o_sent.at[d, j], o_got.at[d, j],
            on_key_axis(1 - c, d + 1, c),
        )

    def l_copy(d, j):
        return remote(
            lsend.at[d, j], lrecv.at[d, j], l_sent.at[d, j], l_got.at[d, j],
            on_key_axis(1 - c, d + 1, c),
        )

    def last(j, carry):
        for d in (1, 0, 2, 3):
            total, new = attend(KSTEPS - 1, lax.rem(qpos + d + 1, 4), j)
            summed = total[:, HD:]
            o = total[:, :HD] / summed
            lse = new * SCALE + jnp.log2(summed)
            if d == 3:
                oown[j] = o
                lown[j] = lse
            else:
                osend[d, j] = o.astype(BF16).reshape(HB, CH, HD)
                lsend[d, j] = jnp.sum(
                    jnp.where(eye[None], lse.reshape(ROWS // HD, HD, HD), 0.0), axis=1
                )
                o_copy(d, j).start()
                l_copy(d, j).start()
        return carry

    lax.fori_loop(0, 2, lambda i, carry: last(1 - i, carry), 0)

    r_dst = cols(out_ref, z)

    def r_copy(j, i):
        z2 = source(j * HB + i)
        return remote(zsend.at[j, i], r_dst, r_sent.at[j, i], r_got, dev(z2=z2))

    def combine(j, carry):
        parts = [oown[j]]
        weights = [lown[j]]
        for d in range(3):
            o_copy(d, j).wait_recv()
            l_copy(d, j).wait_recv()
            stat = lrecv[d, j]
            wide = jnp.sum(
                jnp.where(eye[None], jnp.broadcast_to(stat[:, None, :], (ROWS // HD, HD, HD)), 0.0),
                axis=2, keepdims=True,
            )
            weights.append(jnp.broadcast_to(wide, (ROWS // HD, HD, HD)).reshape(ROWS, HD))
            parts.append(orecv[d, j].reshape(ROWS, HD).astype(F32))
        high = functools.reduce(jnp.maximum, weights)
        weights = [jnp.exp2(w - high) for w in weights]
        mixed = sum(w * o for w, o in zip(weights, parts)) / sum(weights)
        zsend[j] = mixed.astype(BF16).reshape(HB, CH, HD)

        def home(i, carry2):
            r_copy(j, HB - 1 - i).start()
            return carry2

        lax.fori_loop(0, HB - 1 + j, home, 0)
        return carry

    combine(1, 0)
    combine(0, 0)
    pltpu.make_async_copy(zsend.at[0, 0], r_dst, r_got).start()
    wait_bytes(out_ref, r_got)

    lax.fori_loop(1, NZ, sent_q, 0)
    lax.fori_loop(1, NZ, sent_kv, 0)
    def drain_y(n, carry):
        for dy in (2, 1, 3):
            y_copy(n, dy).wait_send()
        return carry

    lax.fori_loop(0, STEPS, drain_y, 0)

    for n in range(KSTEPS):
        for copy in across(n):
            copy.wait_send()

    def drain_o(j, carry):
        for d in range(3):
            o_copy(d, j).wait_send()
            l_copy(d, j).wait_send()
        return carry

    lax.fori_loop(0, 2, drain_o, 0)

    def drain_r(i, carry):
        r_copy(i // HB, i % HB).wait_send()
        return carry

    lax.fori_loop(1, NZ, drain_r, 0)


def attention(queries, keys, values, tile_mask, frame_order):
    dma = pltpu.SemaphoreType.DMA
    hbm = pl.BlockSpec(memory_space=pl.ANY)
    return pl.pallas_call(
        kernel,
        out_shape=jax.ShapeDtypeStruct(queries.shape, BF16),
        in_specs=[hbm] * 5,
        out_specs=hbm,
        scratch_shapes=[
            pltpu.VMEM((2 * NZ, 4, 4, 2 * NZ), jnp.int32),
            pltpu.SMEM((2 * NZ,), jnp.int32),
            pltpu.VMEM((4, NZ, CH, 2 * HD), BF16),
            pltpu.VMEM((NZ, 4, 2, 2, CH, 2 * HD), BF16),
            pltpu.VMEM((4, NZ, CH, 2 * HD), F32),
            pltpu.VMEM((4, NZ, CH, HD), F32),
            pltpu.VMEM((3, 2, NZ // 2, CH, HD), BF16),
            pltpu.VMEM((3, 2, 2, HD), F32),
            pltpu.VMEM((3, 2, NZ // 2, CH, HD), BF16),
            pltpu.VMEM((3, 2, 2, HD), F32),
            pltpu.VMEM((2, NZ // 2 * CH, HD), F32),
            pltpu.VMEM((2, NZ // 2 * CH, HD), F32),
            pltpu.VMEM((2, NZ // 2, CH, HD), BF16),
            dma((NZ,)), dma((NZ,)), dma((NZ,)),
            dma((STEPS,)), dma((KSTEPS,)),
            dma((STEPS, 4)), dma((STEPS, 4)),
            dma((KSTEPS, 8)), dma((KSTEPS, 4)), dma((KSTEPS,)),
            dma((3, 2)), dma((3, 2)), dma((3, 2)), dma((3, 2)),
            dma((2, NZ // 2)), dma, dma((2,)),
        ],
        compiler_params=pltpu.CompilerParams(
            collective_id=0, has_side_effects=True, vmem_limit_bytes=56 * 2**20
        ),
        name="attention",
    )(queries, keys, values, tile_mask, frame_order)


def per_device(queries, keys, values, tile_mask, frame_order):
    by_key = jnp.transpose(tile_mask, (0, 2, 3, 1))
    return attention(queries, keys, values, by_key, frame_order)


def solution(mesh):
    rows = P(("blk", "uly"), None)
    return jax.shard_map(
        per_device,
        mesh=mesh,
        in_specs=(rows, rows, rows, P(), P()),
        out_specs=rows,
        check_vma=False,
    )
```
